32 devices in a mesh: groups: 2 (over y), blocks: 4 (over z), views: 2 (over x), sub: 2 (over core).
Axes of the slice: x: 2, y: 2, z: 4, core: 2. Of those that a mesh axis runs over, the one named last changes fastest.
Arguments:
- estimate0: float32 [128, 32, 512], P(('groups', 'blocks'), 'sub', 'views'), parts along dimension 0, may hold values from 0.25 to 4
- measured: bfloat16 [8, 2, 2048, 512], P('views', 'sub', ('groups', 'blocks')), parts along dimension 2, may hold values from 0.19921875 to 5
- line_target: int32 [8, 2, 2048], P('views', 'sub', ('groups', 'blocks')), parts along dimension 2, may hold values from 0 to 1023, as said below
- band: int32 [8, 64], replicated, may hold values from 0 to 7
- psf: float32 [8, 8, 17], replicated, may hold values from 0.02 to 0.12
- background: float32 [8], replicated, may hold values from 0.1 to 1
Outputs:
- estimate: float32 [128, 32, 512], P(('groups', 'blocks'), 'sub', 'views'), parts along dimension 0
The draws below stay inside these ranges and needn't reach their ends.
There are 2 independent parts, one for each index of `groups`. The reference program is written for one: setup_inputs(seed, part) draws one part's arguments, and reference() takes and returns one part's arrays. A program takes and returns all parts, laid end to end along the dimension named above; an argument that names none is the same for every part. Nothing has to cross between parts.
Inputs may be any that keep to these rules, and one draw needn't show every extreme that they name: For each view v and y range h, line_target[v, h] is a permutation of 0 .. 1023. The lines held by one device (aligned runs of 256 lines) send at most 128 lines to any one z-block, and this most is reached by every device.
All inputs are finite; a program needn't handle non-finite values.
Results may differ from the reference program's by a relative error of at most 0.0003.
Values may be sent and summed in bfloat16 or wider, within the bound.
A program may use at most 64 MiB of HBM per device.

```python
import math
import jax
import jax.numpy as jnp

NV = 8
NB = 8
HW = 8
TAPS = 17
ITERS = 2
CZ = 16
CY = 16
NX = 512
NY = 32
NZ = 64
HALVES = 2
LINES = 1024
N_BLOCKS = 4


def route_one(key_view):
    blocks_count = N_BLOCKS
    per_block = CZ * CY
    mean_count = per_block // blocks_count
    key_share, key_inner, key_order = jax.random.split(key_view, 3)
    index_row = jnp.arange(blocks_count, dtype=jnp.int32)
    profile = jnp.where(index_row < blocks_count // 4, 2 * mean_count, jnp.where(index_row < blocks_count // 2, mean_count, mean_count // 2))
    share = profile[jax.random.permutation(key_share, blocks_count)]
    counts = share[(index_row[None, :] - index_row[:, None]) % blocks_count]
    before = jnp.cumsum(counts, axis=0) - counts
    ends = jnp.cumsum(counts, axis=1)
    starts = ends - counts
    line_ids = jnp.arange(per_block, dtype=jnp.int32)
    destination = jnp.sum((line_ids[None, :, None] >= ends[:, None, :]).astype(jnp.int32), axis=2)
    rank_in = line_ids[None, :] - jnp.take_along_axis(starts, destination, axis=1)
    slot_index = jnp.take_along_axis(before, destination, axis=1) + rank_in
    inner = jax.vmap(lambda single: jax.random.permutation(single, per_block))(jax.random.split(key_inner, blocks_count))
    local_line = inner[destination, slot_index]
    target = destination * per_block + local_line
    order = jax.vmap(lambda single: jax.random.permutation(single, per_block))(jax.random.split(key_order, blocks_count))
    target = jnp.take_along_axis(target, order, axis=1)
    return target.reshape(-1).astype(jnp.int32)


def draw_line_target(key, part):
    key = jax.random.fold_in(key, 7)
    keys_all = jax.random.split(key, NV * HALVES)
    routed = jax.vmap(route_one)(keys_all)
    return routed.reshape(NV, HALVES, LINES).astype(jnp.int32)


def plant(values, stream_key, smallest, high):
    dims = values.shape
    index_at = [jax.random.randint(jax.random.fold_in(stream_key, axis), (), 0, dims[axis]) for axis in range(len(dims))]
    values = values.at[tuple(index_at)].set(smallest)
    longest = dims.index(max(dims))
    index_at[longest] = (index_at[longest] + 1) % dims[longest]
    return values.at[tuple(index_at)].set(high)


def level_of(rng, extent, shards, least, largest):
    factor_of = 1.0
    for position, blocks in shards:
        draws = jax.random.uniform(jax.random.fold_in(jax.random.fold_in(rng, 6), position), (blocks,), jnp.float32, least / len(shards), largest / len(shards))
        factor_of = factor_of * jnp.repeat(jnp.exp(draws), extent[position] // blocks).reshape((-1,) + (1,) * (len(extent) - 1 - position))
    return factor_of


def setup_inputs(seed: int = 0, part: int = 0) -> dict:
    key_list = jax.random.split(jax.random.key(seed), 7)
    part_keys = jax.random.split(jax.random.fold_in(key_list[6], part), 7)
    return {
        "estimate0": jnp.clip(jnp.exp(math.log(4.0) - 2.7725887 * jax.random.uniform(part_keys[0], (NZ, NY, NX), jnp.float32) ** level_of(part_keys[0], (NZ, NY, NX), ((0, 4), (1, 2), (2, 2)), -0.2, 0.2)), 0.25, 4.0),
        "measured": jnp.clip(jnp.exp(math.log(5.0) - 3.2227897 * jax.random.uniform(part_keys[1], (NV, HALVES, LINES, NX), jnp.float32) ** level_of(part_keys[1], (NV, HALVES, LINES, NX), ((0, 2), (1, 2), (2, 4)), -0.2, 0.2)), 0.19921875, 5.0).astype(jnp.bfloat16),
        "line_target": draw_line_target(jax.random.fold_in(jax.random.fold_in(key_list[6], part), 71), part),
        "band": plant(jax.random.randint(key_list[3], (NV, NZ), 0, NB), jax.random.fold_in(key_list[3], 1), 0, NB - 1).astype(jnp.int32),
        "psf": jnp.clip(jnp.exp(jax.random.uniform(key_list[4], (NV, NB, TAPS), jnp.float32, math.log(0.02), math.log(0.12))), 0.02, 0.12),
        "background": jnp.clip(jnp.exp(jax.random.uniform(key_list[5], (NV,), jnp.float32, math.log(0.1), math.log(1.0))), 0.1, 1.0),
    }


def pick_rows(psf_view, band_view):
    return psf_view[band_view]


def blur_field(field, coef):
    padded = jnp.pad(field, ((HW, HW), (0, 0), (0, 0)))
    total = jnp.zeros(field.shape, jnp.float32)
    for tap in range(TAPS):
        total = total + coef[:, tap, None, None] * padded[tap:tap + NZ]
    return total


def back_field(field, coef):
    padded = jnp.pad(field, ((HW, HW), (0, 0), (0, 0)))
    coef_pad = jnp.pad(coef, ((HW, HW), (0, 0)))
    total = jnp.zeros(field.shape, jnp.float32)
    for tap in range(TAPS):
        lower = 2 * HW - tap
        total = total + coef_pad[lower:lower + NZ, tap, None, None] * padded[lower:lower + NZ]
    return total


def place_lines(rows_in, targets):
    return jnp.zeros((LINES, NX), jnp.bfloat16).at[targets].set(rows_in)


def reference(estimate0, measured, line_target, band, psf, background):
    coef_all = jax.vmap(pick_rows)(psf, band)
    norm_sum = jnp.zeros((NZ, 1, 1), jnp.float32)
    for view in range(NV):
        norm_sum = norm_sum + back_field(jnp.ones((NZ, 1, 1), jnp.float32), coef_all[view])
    observed = []
    for view in range(NV):
        lines = jax.vmap(place_lines)(measured[view], line_target[view])
        lines = lines.reshape(HALVES, NZ, CY, NX).transpose(1, 0, 2, 3).reshape(NZ, NY, NX)
        observed.append(lines)
    estimate = estimate0
    for sweep in range(ITERS):
        total = jnp.zeros(estimate.shape, jnp.float32)
        for view in range(NV):
            forward = background[view] + blur_field(estimate, coef_all[view])
            ratio = observed[view].astype(jnp.float32) / forward
            total = total + back_field(ratio, coef_all[view])
        estimate = estimate * total / norm_sum
    return estimate
```

```python
import functools

import jax
import jax.numpy as jnp
from jax import lax
from jax.experimental import pallas as pl
from jax.experimental.pallas import tpu as pltpu
from jax.sharding import PartitionSpec as P

ITERS = 2
HW = 8
CHUNKS = 4
MESH = pl.DeviceIdType.MESH
f32, bf16 = jnp.float32, jnp.bfloat16


def xor(a, b, size):
    out, bit = 0, 1
    while bit < size:
        p, q = (a // bit) % 2, (b // bit) % 2
        out = out + bit * (p + q - 2 * p * q)
        bit *= 2
    return out


def split3(value, axis):
    hi = value.astype(bf16)
    lo = (value - hi.astype(f32)).astype(bf16)
    return jnp.concatenate([hi, lo, hi], axis=axis)


def weights3(rep, width):
    hi = rep.astype(bf16)
    lo = rep - hi.astype(f32)
    lane = lax.broadcasted_iota(jnp.int32, rep.shape, 1)
    return jnp.where(lane < 2 * width, hi.astype(f32), lo).astype(bf16)


def kernel(
    nb, nv, est_in, meas, targ, f_rep, b_rep, norm, bg, out,
    packed, idsend, recv, idrecv, obs, fwd, est0, est1, share, hal, spout, spin, f3, b3,
    data_send, data_recv, id_send, id_recv, own_sem, hal_send, hal_recv,
):
    vc, lines, width = meas.shape
    rows, depth, xl = est0.shape
    cap = 2 * lines // nb
    n = nb * nv
    per = rows // CHUNKS
    my_b, my_g = lax.axis_index("blocks"), lax.axis_index("views")
    has_prev, has_next = my_b > 0, my_b < nb - 1

    def each(body):
        if n <= 16:
            for i in range(n - 1):
                body(n - 1 - i)
        else:
            def step(i, carry):
                body(n - 1 - i)
                return carry
            lax.fori_loop(0, n - 1, step, 0)

    def peer(o):
        return xor(my_b, o // nv, nb), xor(my_g, o % nv, nv)

    barrier = pltpu.get_barrier_semaphore()

    def greet(o):
        b, g = peer(o)
        pl.semaphore_signal(
            barrier, inc=1, device_id={"blocks": b, "views": g}, device_id_type=MESH
        )

    each(greet)

    idsend[...] = jnp.zeros_like(idsend)
    high = max(16, nb)
    before = (
        lax.broadcasted_iota(jnp.int32, (lines, lines), 0)
        < lax.broadcasted_iota(jnp.int32, (lines, lines), 1)
    )
    before = jnp.where(before, 1.0, 0.0).astype(bf16)
    block_of = lax.broadcasted_iota(jnp.int32, (high, lines), 0)
    slot_of = lax.broadcasted_iota(jnp.int32, (nb * cap, lines), 0).astype(f32)
    for v in range(vc):
        t = targ[v]
        inside = (t >= block_of * lines) & (t < (block_of + 1) * lines)
        member = jnp.where(inside, 1.0, 0.0)
        rank = jnp.dot(member.astype(bf16), before, preferred_element_type=f32)
        place = rank + (block_of * cap).astype(f32)
        slot = jnp.sum(member * place, axis=0, keepdims=True)
        first = jnp.sum(member * (block_of * lines).astype(f32), axis=0, keepdims=True)
        local = t - first.astype(jnp.int32)
        shift = rows.bit_length() - 1
        line = (local & (rows - 1)) * depth + (local >> shift)
        pick = jnp.where(slot_of == slot, 1.0, 0.0).astype(bf16)
        moved = jnp.dot(pick, meas[v], preferred_element_type=f32).astype(bf16)
        for b in range(nb):
            for g in range(nv):
                packed[b, g, v * cap:(v + 1) * cap, :] = moved[
                    b * cap:(b + 1) * cap, g * xl:(g + 1) * xl
                ]
        ids = jnp.broadcast_to((line + 1).astype(f32), (16, lines)).astype(bf16)
        ids = lax.dot_general(
            ids, pick, (((1,), (1,)), ((), ())), preferred_element_type=f32
        )
        for b in range(nb):
            idsend[b, v:v + 1, :cap] = ids[0:1, b * cap:(b + 1) * cap]

    for y in range(rows):
        est0[y] = est_in[:, y, :]

    pl.semaphore_wait(barrier, n - 1)

    def copies(o):
        b, g = peer(o)
        to = {"blocks": b, "views": g}
        return (
            pltpu.make_async_remote_copy(
                src_ref=packed.at[b, g], dst_ref=recv.at[o], send_sem=data_send.at[o],
                recv_sem=data_recv.at[o], device_id=to, device_id_type=MESH,
            ),
            pltpu.make_async_remote_copy(
                src_ref=idsend.at[b], dst_ref=idrecv.at[o], send_sem=id_send.at[o],
                recv_sem=id_recv.at[o], device_id=to, device_id_type=MESH,
            ),
        )

    def halo(phase, c, src_up, dst_up, src_down, dst_down):
        up = pltpu.make_async_remote_copy(
            src_ref=src_up, dst_ref=dst_up, send_sem=hal_send.at[phase, 0, c],
            recv_sem=hal_recv.at[phase, 0, c],
            device_id={"blocks": lax.rem(my_b + 1, nb)}, device_id_type=MESH,
        )
        down = pltpu.make_async_remote_copy(
            src_ref=src_down, dst_ref=dst_down, send_sem=hal_send.at[phase, 1, c],
            recv_sem=hal_recv.at[phase, 1, c],
            device_id={"blocks": lax.rem(my_b + nb - 1, nb)}, device_id_type=MESH,
        )

        def start():
            pl.when(has_next)(up.start)
            pl.when(has_prev)(down.start)

        def arrived():
            pl.when(has_prev)(up.wait_recv)
            pl.when(has_next)(down.wait_recv)

        def sent():
            pl.when(has_next)(up.wait_send)
            pl.when(has_prev)(down.wait_send)

        return start, arrived, sent

    def est_halo(sweep, c):
        if sweep == 0:
            est, ys = est0, pl.ds(0, rows)
        else:
            est, ys = est1, pl.ds(c * per, per)
        return halo(
            2 * sweep, c,
            est.at[ys, depth - HW:depth, :], hal.at[sweep, 0, ys],
            est.at[ys, 0:HW, :], hal.at[sweep, 1, ys],
        )

    def sp_halo(sweep, c):
        ys = pl.ds(c * per, per)
        return halo(
            2 * sweep + 1, c,
            spout.at[sweep, 1, ys], spin.at[sweep, 0, ys],
            spout.at[sweep, 0, ys], spin.at[sweep, 1, ys],
        )

    est_halo(0, 0)[0]()

    def send(o):
        data, ids = copies(o)
        ids.start()
        data.start()

    each(send)
    own = pltpu.make_async_copy(packed.at[my_b, my_g], recv.at[0], own_sem.at[0])
    own_id = pltpu.make_async_copy(idsend.at[my_b], idrecv.at[0], own_sem.at[1])
    own.start()
    own_id.start()

    @pl.when(my_b == 0)
    def _():
        for s in range(ITERS):
            hal[s, 0] = jnp.zeros_like(hal[s, 0])
            spin[s, 0] = jnp.zeros_like(spin[s, 0])

    @pl.when(my_b == nb - 1)
    def _():
        for s in range(ITERS):
            hal[s, 1] = jnp.zeros_like(hal[s, 1])
            spin[s, 1] = jnp.zeros_like(spin[s, 1])

    obs[...] = jnp.zeros_like(obs)
    window = depth + 2 * HW
    f3[...] = weights3(f_rep[...], window)
    b3[...] = weights3(b_rep[...], bg.shape[0])
    level = jnp.broadcast_to(bg[...], (bg.shape[0], xl))

    def project(sweep, est, y):
        field = jnp.concatenate([hal[sweep, 0, y], est[y], hal[sweep, 1, y]], axis=0)
        return jnp.dot(f3[...], split3(field, 0), preferred_element_type=f32) + level

    def loop(count, body):
        def step(i, carry):
            body(i)
            return carry
        lax.fori_loop(0, count, step, 0)

    est_halo(0, 0)[1]()

    def first_forward(c):
        for j in range(per):
            y = c * per + j
            fwd[y] = project(0, est0, y)

    loop(CHUNKS, first_forward)

    row_of = (lax.broadcasted_iota(jnp.int32, (lines, cap), 0) + 1).astype(f32)

    def put(o):
        g = xor(my_g, o % nv, nv)
        for v in range(vc):
            pick = jnp.where(idrecv[o, v:v + 1, :cap] == row_of, 1.0, 0.0).astype(bf16)
            found = jnp.dot(
                pick, recv[o, v * cap:(v + 1) * cap, :], preferred_element_type=f32
            ).reshape(rows, depth, xl)
            at = pl.ds(pl.multiple_of((g * vc + v) * depth, depth), depth)
            obs[:, at, :] = obs[:, at, :] + found

    own.wait()
    own_id.wait()
    put(0)

    def take(i):
        data, ids = copies(i)
        ids.wait_recv()
        data.wait_recv()
        put(i)

    if n <= 16:
        for o in range(1, n):
            take(o)
    else:
        loop(n - 1, lambda i: take(i + 1))

    scale = 1.0 / jnp.broadcast_to(norm[...], (depth, xl))
    for sweep in range(ITERS):
        est = est0 if sweep == 0 else est1

        def back(c):
            if sweep > 0:
                est_halo(sweep, c)[1]()
            for j in range(per):
                y = c * per + j
                forward = fwd[y] if sweep == 0 else project(sweep, est, y)
                ratio = obs[y] / forward
                spread = jnp.dot(b3[...], split3(ratio, 0), preferred_element_type=f32)
                spout[sweep, 0, y] = spread[:HW]
                share[y] = spread[HW:HW + depth]
                spout[sweep, 1, y] = spread[HW + depth:]
            sp_halo(sweep, c)[0]()

        def update(c):
            sp_halo(sweep, c)[1]()
            for j in range(per):
                y = c * per + j
                total = share[y] + jnp.concatenate(
                    [spin[sweep, 0, y], spin[sweep, 1, y]], axis=0
                )
                value = est[y] * (total * scale)
                if sweep == 0:
                    est1[y] = value
                else:
                    share[y] = value
            if sweep == 0:
                est_halo(1, c)[0]()

        loop(CHUNKS, back)
        loop(CHUNKS, update)
    for y in range(rows):
        out[:, y, :] = share[y]

    def done(o):
        data, ids = copies(o)
        ids.wait_send()
        data.wait_send()

    each(done)
    est_halo(0, 0)[2]()

    def last(c):
        sp_halo(0, c)[2]()
        est_halo(1, c)[2]()
        sp_halo(1, c)[2]()

    loop(CHUNKS, last)


def shards(nb, nv, estimate0, measured, line_target, band, psf, background):
    depth, rows, xl = estimate0.shape
    vc, _, lines, width = measured.shape
    taps, views = psf.shape[2], psf.shape[0]
    assert depth == 2 * HW and taps == 2 * HW + 1 and lines == rows * depth <= 256
    window = depth + 2 * HW
    cap = 2 * lines // nb
    n = nb * nv
    highest = lax.Precision.HIGHEST
    start = lax.axis_index("blocks") * depth
    offsets = jnp.arange(window, dtype=jnp.int32) + start - HW
    valid = (offsets >= 0) & (offsets < band.shape[1])
    padded = jnp.pad(band, ((0, 0), (HW, HW)), mode="edge")
    near = lax.dynamic_slice_in_dim(padded, start, window, 1)
    onehot = (
        (near[:, :, None] == jnp.arange(psf.shape[1], dtype=jnp.int32)) & valid[None, :, None]
    ).astype(f32)
    coef = jnp.einsum("vwb,vbk->vwk", onehot, psf, precision=highest)
    z = jnp.arange(depth, dtype=jnp.int32)
    w = jnp.arange(window, dtype=jnp.int32)
    k = jnp.arange(taps, dtype=jnp.int32)
    forward_pick = (w[None, :, None] - z[:, None, None] == k).astype(f32)
    backward_pick = (z[None, :, None] - w[:, None, None] + 2 * HW == k).astype(f32)
    norm = jnp.einsum("vwk,wck->c", coef, backward_pick, precision=highest)
    mat = jnp.einsum("vzk,zwk->vzw", coef[:, HW:HW + depth], forward_pick, precision=highest)
    mat = mat.reshape(views * depth, window)
    f_rep = jnp.concatenate([mat] * 3, axis=1)
    b_rep = jnp.concatenate([mat.T] * 3, axis=1)
    bg = jnp.repeat(background, depth)[:, None]
    vz = views * depth
    vmem = pl.BlockSpec(memory_space=pltpu.VMEM)
    dma = pltpu.SemaphoreType.DMA
    return pl.pallas_call(
        functools.partial(kernel, nb, nv),
        out_shape=jax.ShapeDtypeStruct((depth, rows, xl), f32),
        in_specs=[vmem] * 7,
        out_specs=vmem,
        scratch_shapes=[
            pltpu.VMEM((nb, nv, vc * cap, xl), bf16),
            pltpu.VMEM((nb, 8, 128), f32),
            pltpu.VMEM((n, vc * cap, xl), bf16),
            pltpu.VMEM((n, 8, 128), f32),
            pltpu.VMEM((rows, vz, xl), f32),
            pltpu.VMEM((rows, vz, xl), f32),
            pltpu.VMEM((rows, depth, xl), f32),
            pltpu.VMEM((rows, depth, xl), f32),
            pltpu.VMEM((rows, depth, xl), f32),
            pltpu.VMEM((ITERS, 2, rows, HW, xl), f32),
            pltpu.VMEM((ITERS, 2, rows, HW, xl), f32),
            pltpu.VMEM((ITERS, 2, rows, HW, xl), f32),
            pltpu.VMEM((vz, 3 * window), bf16),
            pltpu.VMEM((window, 3 * vz), bf16),
            dma((n,)),
            dma((n,)),
            dma((n,)),
            dma((n,)),
            dma((2,)),
            dma((2 * ITERS, 2, CHUNKS)),
            dma((2 * ITERS, 2, CHUNKS)),
        ],
        compiler_params=pltpu.CompilerParams(
            collective_id=0, has_side_effects=True, vmem_limit_bytes=48 << 20
        ),
    )(estimate0, measured[:, 0], line_target, f_rep, b_rep, norm[:, None], bg)


def solution(mesh):
    in_specs = (
        P(("groups", "blocks"), "sub", "views"),
        P("views", "sub", ("groups", "blocks"), None),
        P("views", "sub", ("groups", "blocks")),
        P(),
        P(),
        P(),
    )
    out_specs = P(("groups", "blocks"), "sub", "views")
    body = functools.partial(shards, mesh.shape["blocks"], mesh.shape["views"])
    return jax.shard_map(body, mesh=mesh, in_specs=in_specs, out_specs=out_specs, check_vma=False)
```

```python
import functools

import jax
import jax.numpy as jnp
from jax import lax
from jax.experimental import pallas as pl
from jax.experimental.pallas import tpu as pltpu
from jax.sharding import PartitionSpec as P

ITERS = 2
HW = 8
CHUNKS = 4
MESH = pl.DeviceIdType.MESH
f32, bf16 = jnp.float32, jnp.bfloat16


def xor(a, b, size):
    out, bit = 0, 1
    while bit < size:
        p, q = (a // bit) % 2, (b // bit) % 2
        out = out + bit * (p + q - 2 * p * q)
        bit *= 2
    return out


def split3(value, axis):
    hi = value.astype(bf16)
    lo = (value - hi.astype(f32)).astype(bf16)
    return jnp.concatenate([hi, lo, hi], axis=axis)


def kernel(
    nb, nv, est_in, meas, targ, band, psf, bg, out,
    packed, idsend, recv, idrecv, obs, fwd, est0, est1, share, hal, spout, spin, f3, b3, b3s, coefs, acc,
    data_send, data_recv, id_send, id_recv, own_sem, hal_send, hal_recv,
):
    vc, lines, width = meas.shape
    rows, depth, xl = est0.shape
    cap = 2 * lines // nb
    n = nb * nv
    per = rows // CHUNKS
    my_b, my_g = lax.axis_index("blocks"), lax.axis_index("views")
    has_prev, has_next = my_b > 0, my_b < nb - 1

    def each(body):
        if n <= 16:
            for i in range(n - 1):
                body(n - 1 - i)
        else:
            def step(i, carry):
                body(n - 1 - i)
                return carry
            lax.fori_loop(0, n - 1, step, 0)

    def peer(o):
        return xor(my_b, o // nv, nb), xor(my_g, o % nv, nv)

    barrier = pltpu.get_barrier_semaphore()

    def greet(o):
        b, g = peer(o)
        pl.semaphore_signal(
            barrier, inc=1, device_id={"blocks": b, "views": g}, device_id_type=MESH
        )

    each(greet)

    idsend[...] = jnp.zeros_like(idsend)
    high = max(16, nb)
    before = (
        lax.broadcasted_iota(jnp.int32, (lines, lines), 0)
        < lax.broadcasted_iota(jnp.int32, (lines, lines), 1)
    )
    before = jnp.where(before, 1.0, 0.0).astype(bf16)
    block_of = lax.broadcasted_iota(jnp.int32, (high, lines), 0)
    slot_of = lax.broadcasted_iota(jnp.int32, (nb * cap, lines), 0).astype(f32)
    def pack(v):
        t = targ[v]
        inside = (t >= block_of * lines) & (t < (block_of + 1) * lines)
        member = jnp.where(inside, 1.0, 0.0)
        rank = jnp.dot(member.astype(bf16), before, preferred_element_type=f32)
        place = rank + (block_of * cap).astype(f32)
        slot = jnp.sum(member * place, axis=0, keepdims=True)
        first = jnp.sum(member * (block_of * lines).astype(f32), axis=0, keepdims=True)
        local = t - first.astype(jnp.int32)
        shift = rows.bit_length() - 1
        line = (local & (rows - 1)) * depth + (local >> shift)
        pick = jnp.where(slot_of == slot, 1.0, 0.0).astype(bf16)
        moved = jnp.dot(pick, meas[v], preferred_element_type=f32).astype(bf16)
        for b in range(nb):
            for g in range(nv):
                packed[b, g, v * cap:(v + 1) * cap, :] = moved[
                    b * cap:(b + 1) * cap, g * xl:(g + 1) * xl
                ]
        ids = jnp.broadcast_to((line + 1).astype(f32), (16, lines)).astype(bf16)
        ids = lax.dot_general(
            ids, pick, (((1,), (1,)), ((), ())), preferred_element_type=f32
        )
        for b in range(nb):
            idsend[b, v:v + 1, :cap] = ids[0:1, b * cap:(b + 1) * cap]

    pack(0)
    for y in range(rows):
        est0[y] = est_in[:, y, :]

    pl.semaphore_wait(barrier, n - 1)

    def data_copy(o, v):
        b, g = peer(o)
        at = pl.ds(v * cap, cap)
        return pltpu.make_async_remote_copy(
            src_ref=packed.at[b, g, at], dst_ref=recv.at[o, at], send_sem=data_send.at[o, v],
            recv_sem=data_recv.at[o, v], device_id={"blocks": b, "views": g},
            device_id_type=MESH,
        )

    def id_copy(o):
        b, g = peer(o)
        return pltpu.make_async_remote_copy(
            src_ref=idsend.at[b], dst_ref=idrecv.at[o], send_sem=id_send.at[o],
            recv_sem=id_recv.at[o], device_id={"blocks": b, "views": g},
            device_id_type=MESH,
        )

    def halo(phase, c, src_up, dst_up, src_down, dst_down):
        up = pltpu.make_async_remote_copy(
            src_ref=src_up, dst_ref=dst_up, send_sem=hal_send.at[phase, 0, c],
            recv_sem=hal_recv.at[phase, 0, c],
            device_id={"blocks": lax.rem(my_b + 1, nb)}, device_id_type=MESH,
        )
        down = pltpu.make_async_remote_copy(
            src_ref=src_down, dst_ref=dst_down, send_sem=hal_send.at[phase, 1, c],
            recv_sem=hal_recv.at[phase, 1, c],
            device_id={"blocks": lax.rem(my_b + nb - 1, nb)}, device_id_type=MESH,
        )

        def start():
            pl.when(has_next)(up.start)
            pl.when(has_prev)(down.start)

        def arrived():
            pl.when(has_prev)(up.wait_recv)
            pl.when(has_next)(down.wait_recv)

        def sent():
            pl.when(has_next)(up.wait_send)
            pl.when(has_prev)(down.wait_send)

        return start, arrived, sent

    def est_halo(sweep, c):
        if sweep == 0:
            est, ys = est0, pl.ds(0, rows)
        else:
            est, ys = est1, pl.ds(c * per, per)
        return halo(
            2 * sweep, c,
            est.at[ys, depth - HW:depth, :], hal.at[sweep, 0, ys],
            est.at[ys, 0:HW, :], hal.at[sweep, 1, ys],
        )

    def sp_halo(sweep, c):
        ys = pl.ds(c * per, per)
        return halo(
            2 * sweep + 1, c,
            spout.at[sweep, 1, ys], spin.at[sweep, 0, ys],
            spout.at[sweep, 0, ys], spin.at[sweep, 1, ys],
        )

    each(lambda o: data_copy(o, 0).start())
    est_halo(0, 0)[0]()
    for v in range(1, vc):
        pack(v)
        if v == vc - 1:
            each(lambda o: id_copy(o).start())
        each(lambda o: data_copy(o, v).start())
    own = pltpu.make_async_copy(packed.at[my_b, my_g], recv.at[0], own_sem.at[0])
    own_id = pltpu.make_async_copy(idsend.at[my_b], idrecv.at[0], own_sem.at[1])
    own.start()
    own_id.start()

    @pl.when(my_b == 0)
    def _():
        for s in range(ITERS):
            hal[s, 0] = jnp.zeros_like(hal[s, 0])
            spin[s, 0] = jnp.zeros_like(spin[s, 0])

    @pl.when(my_b == nb - 1)
    def _():
        for s in range(ITERS):
            hal[s, 1] = jnp.zeros_like(hal[s, 1])
            spin[s, 1] = jnp.zeros_like(spin[s, 1])

    obs[...] = jnp.zeros_like(obs)
    window = depth + 2 * HW
    views, bands, taps = psf.shape
    order = [g * vc + v for v in range(vc) for g in range(nv)]
    nz = band.shape[1]
    iota = functools.partial(lax.broadcasted_iota, jnp.int32)

    in_band = jnp.concatenate(
        [jnp.broadcast_to(band[v:v + 1, :], (bands, nz)) for v in range(views)], axis=0
    ) == lax.rem(iota((views * bands, nz), 0), bands)
    in_band = jnp.where(in_band, 1.0, 0.0).astype(bf16)
    reach = iota((window, nz), 1) - iota((window, nz), 0) == my_b * depth - HW
    reach = jnp.where(reach, 1.0, 0.0).astype(bf16)
    near = lax.dot_general(
        reach, in_band, (((1,), (1,)), ((), ())), preferred_element_type=f32
    )
    lane_view = iota(near.shape, 1) // bands
    near = jnp.concatenate(
        [jnp.where(lane_view == v, near, 0.0) for v in range(views)], axis=0
    ).astype(bf16)
    table = psf[...].reshape(views * bands, taps)
    found = None
    for _ in range(3):
        part = table.astype(bf16)
        table = table - part.astype(f32)
        term = jnp.dot(near, part, preferred_element_type=f32)
        found = term if found is None else found + term
    coefs[...] = jnp.zeros_like(coefs)
    for v in range(views):
        coefs[v, :, :taps] = found[v * window:(v + 1) * window]

    centre = jnp.concatenate([coefs[v, HW:HW + depth, :] for v in order], axis=0)
    row_z = lax.rem(iota(centre.shape, 0), depth)
    mat = jnp.where(row_z == 0, centre, 0.0)
    for z in range(1, depth):
        mat = mat + jnp.where(row_z == z, pltpu.roll(centre, z, 1), 0.0)
    hi = mat.astype(bf16).astype(f32)
    lo = (mat - hi).astype(bf16).astype(f32)
    triple = hi + pltpu.roll(hi, window, 1) + pltpu.roll(lo, 2 * window, 1)
    f3[...] = triple[:, :3 * window].astype(bf16)
    hi_t, lo_t = hi.T[:window], lo.T[:window]
    b3[...] = jnp.concatenate([hi_t, hi_t, lo_t], axis=1).astype(bf16)
    part_rows = nv * depth
    for v in range(vc):
        at = slice(v * part_rows, (v + 1) * part_rows)
        pad = jnp.zeros((-3 * part_rows % 128, 128), f32)
        stack = jnp.concatenate([hi[at], hi[at], lo[at], pad], axis=0)
        b3s[v] = stack.T[:window, :3 * part_rows].astype(bf16)

    both = coefs[0]
    for v in range(1, views):
        both = both + coefs[v]
    place_sum = iota(both.shape, 0) + iota(both.shape, 1)
    norm = jnp.zeros((depth, xl), f32)
    for z in range(depth):
        only = jnp.where(place_sum == z + 2 * HW, both, 0.0)
        only = jnp.sum(jnp.sum(only, axis=0, keepdims=True), axis=1, keepdims=True)
        norm = jnp.where(iota((depth, xl), 0) == z, only, norm)
    scale = 1.0 / norm
    level = jnp.concatenate([jnp.full((depth, xl), bg[v], f32) for v in order], axis=0)

    def project(sweep, est, y):
        field = jnp.concatenate([hal[sweep, 0, y], est[y], hal[sweep, 1, y]], axis=0)
        return jnp.dot(f3[...], split3(field, 0), preferred_element_type=f32) + level

    def loop(count, body):
        def step(i, carry):
            body(i)
            return carry
        lax.fori_loop(0, count, step, 0)

    est_halo(0, 0)[1]()

    def first_forward(c):
        for j in range(per):
            y = c * per + j
            fwd[y] = project(0, est0, y)

    loop(CHUNKS, first_forward)

    row_of = (lax.broadcasted_iota(jnp.int32, (lines, cap), 0) + 1).astype(f32)

    def put(o, v):
        g = xor(my_g, o % nv, nv)
        pick = jnp.where(idrecv[o, v:v + 1, :cap] == row_of, 1.0, 0.0).astype(bf16)
        found = jnp.dot(
            pick, recv[o, v * cap:(v + 1) * cap, :], preferred_element_type=f32
        ).reshape(rows, depth, xl)
        at = pl.ds(pl.multiple_of((v * nv + g) * depth, depth), depth)
        obs[:, at, :] = obs[:, at, :] + found

    def partial_back(v, y):
        at = slice(v * part_rows, (v + 1) * part_rows)
        ratio = obs[y, at, :] / fwd[y, at, :]
        part = jnp.dot(b3s[v], split3(ratio, 0), preferred_element_type=f32)
        return part if v == 0 else acc[y] + part

    own.wait()
    own_id.wait()
    for v in range(vc):
        def take(o):
            if v == 0:
                id_copy(o).wait_recv()
            data_copy(o, v).wait_recv()
            put(o, v)

        put(0, v)
        each(take)
        if v < vc - 1:
            def add(c):
                for j in range(per):
                    acc[c * per + j] = partial_back(v, c * per + j)

            loop(CHUNKS, add)

    for sweep in range(ITERS):
        est = est0 if sweep == 0 else est1

        def back(c):
            if sweep > 0:
                est_halo(sweep, c)[1]()
            for j in range(per):
                y = c * per + j
                if sweep == 0:
                    spread = partial_back(vc - 1, y)
                else:
                    ratio = obs[y] / project(sweep, est, y)
                    spread = jnp.dot(b3[...], split3(ratio, 0), preferred_element_type=f32)
                spout[sweep, 0, y] = spread[:HW]
                share[y] = spread[HW:HW + depth]
                spout[sweep, 1, y] = spread[HW + depth:]
            sp_halo(sweep, c)[0]()

        def update(c):
            sp_halo(sweep, c)[1]()
            for j in range(per):
                y = c * per + j
                total = share[y] + jnp.concatenate(
                    [spin[sweep, 0, y], spin[sweep, 1, y]], axis=0
                )
                value = est[y] * (total * scale)
                if sweep == 0:
                    est1[y] = value
                else:
                    share[y] = value
            if sweep == 0:
                est_halo(1, c)[0]()

        loop(CHUNKS, back)
        loop(CHUNKS, update)
    for y in range(rows):
        out[:, y, :] = share[y]

    def done(o):
        id_copy(o).wait_send()
        for v in range(vc):
            data_copy(o, v).wait_send()

    each(done)
    est_halo(0, 0)[2]()

    def last(c):
        sp_halo(0, c)[2]()
        est_halo(1, c)[2]()
        sp_halo(1, c)[2]()

    loop(CHUNKS, last)


def shards(nb, nv, estimate0, measured, line_target, band, psf, background):
    depth, rows, xl = estimate0.shape
    vc, _, lines, width = measured.shape
    taps, views = psf.shape[2], psf.shape[0]
    assert depth == 2 * HW and taps == 2 * HW + 1 and lines == rows * depth <= 256
    window = depth + 2 * HW
    cap = 2 * lines // nb
    n = nb * nv
    assert views * depth == 128 and 3 * window <= 128 and vc <= 8 and cap <= 128
    vz = views * depth
    vmem = pl.BlockSpec(memory_space=pltpu.VMEM)
    dma = pltpu.SemaphoreType.DMA
    return pl.pallas_call(
        functools.partial(kernel, nb, nv),
        out_shape=jax.ShapeDtypeStruct((depth, rows, xl), f32),
        in_specs=[vmem] * 5 + [pl.BlockSpec(memory_space=pltpu.SMEM)],
        out_specs=vmem,
        scratch_shapes=[
            pltpu.VMEM((nb, nv, vc * cap, xl), bf16),
            pltpu.VMEM((nb, 8, 128), f32),
            pltpu.VMEM((n, vc * cap, xl), bf16),
            pltpu.VMEM((n, 8, 128), f32),
            pltpu.VMEM((rows, vz, xl), f32),
            pltpu.VMEM((rows, vz, xl), f32),
            pltpu.VMEM((rows, depth, xl), f32),
            pltpu.VMEM((rows, depth, xl), f32),
            pltpu.VMEM((rows, depth, xl), f32),
            pltpu.VMEM((ITERS, 2, rows, HW, xl), f32),
            pltpu.VMEM((ITERS, 2, rows, HW, xl), f32),
            pltpu.VMEM((ITERS, 2, rows, HW, xl), f32),
            pltpu.VMEM((vz, 3 * window), bf16),
            pltpu.VMEM((window, 3 * vz), bf16),
            pltpu.VMEM((vc, window, 3 * nv * depth), bf16),
            pltpu.VMEM((views, window, 128), f32),
            pltpu.VMEM((rows, window, xl), f32),
            dma((n, vc)),
            dma((n, vc)),
            dma((n,)),
            dma((n,)),
            dma((2,)),
            dma((2 * ITERS, 2, CHUNKS)),
            dma((2 * ITERS, 2, CHUNKS)),
        ],
        compiler_params=pltpu.CompilerParams(
            collective_id=0, has_side_effects=True, vmem_limit_bytes=48 << 20
        ),
    )(estimate0, measured[:, 0], line_target, band, psf, background)


def solution(mesh):
    in_specs = (
        P(("groups", "blocks"), "sub", "views"),
        P("views", "sub", ("groups", "blocks"), None),
        P("views", "sub", ("groups", "blocks")),
        P(),
        P(),
        P(),
    )
    out_specs = P(("groups", "blocks"), "sub", "views")
    body = functools.partial(shards, mesh.shape["blocks"], mesh.shape["views"])
    return jax.shard_map(body, mesh=mesh, in_specs=in_specs, out_specs=out_specs, check_vma=False)
```

```python
import functools

import jax
import jax.numpy as jnp
from jax import lax
from jax.experimental import pallas as pl
from jax.experimental.pallas import tpu as pltpu
from jax.sharding import PartitionSpec as P

ITERS = 2
HW = 8
CHUNKS = 4
MESH = pl.DeviceIdType.MESH
f32, bf16 = jnp.float32, jnp.bfloat16


def xor(a, b, size):
    out, bit = 0, 1
    while bit < size:
        p, q = (a // bit) % 2, (b // bit) % 2
        out = out + bit * (p + q - 2 * p * q)
        bit *= 2
    return out


def split3(value, axis):
    hi = value.astype(bf16)
    lo = (value - hi.astype(f32)).astype(bf16)
    return jnp.concatenate([hi, lo, hi], axis=axis)


def kernel(
    nb, nv, est_far, meas_far, targ_far, band_far, psf_far, bg, out,
    packed, idsend, recv, idrecv, obs, fwd, est0, est1, share, hal, spout, spin, f3, b3, b3s, coefs, acc,
    est_in, meas, targ, band, psf, in_sem,
    data_send, data_recv, id_send, id_recv, own_sem, hal_send, hal_recv,
):
    vc, lines, width = meas.shape
    rows, depth, xl = est0.shape
    cap = 2 * lines // nb
    n = nb * nv
    per = rows // CHUNKS
    my_b, my_g = lax.axis_index("blocks"), lax.axis_index("views")
    has_prev, has_next = my_b > 0, my_b < nb - 1

    def each(body):
        if n <= 16:
            for o in sorted(range(1, n), key=lambda o: (o < n // 2, o % nv)):
                body(o)
        else:
            def step(i, carry):
                body(n - 1 - i)
                return carry
            lax.fori_loop(0, n - 1, step, 0)

    def peer(o):
        return xor(my_b, o // nv, nb), xor(my_g, o % nv, nv)

    barrier = pltpu.get_barrier_semaphore()

    def greet(o):
        b, g = peer(o)
        pl.semaphore_signal(
            barrier, inc=1, device_id={"blocks": b, "views": g}, device_id_type=MESH
        )

    each(greet)
    est_load, meas_load, targ_load, band_load, psf_load = [
        pltpu.make_async_copy(source, held, in_sem.at[i])
        for i, (source, held) in enumerate((
            (est_far, est_in), (meas_far, meas), (targ_far, targ), (band_far, band),
            (psf_far, psf),
        ))
    ]
    for load in (targ_load, meas_load, est_load, band_load, psf_load):
        load.start()

    idsend[...] = jnp.zeros_like(idsend)
    high = max(16, nb)
    before = (
        lax.broadcasted_iota(jnp.int32, (lines, lines), 0)
        < lax.broadcasted_iota(jnp.int32, (lines, lines), 1)
    )
    before = jnp.where(before, 1.0, 0.0).astype(bf16)
    block_of = lax.broadcasted_iota(jnp.int32, (high, lines), 0)
    slot_of = lax.broadcasted_iota(jnp.int32, (nb * cap, lines), 0).astype(f32)
    targ_load.wait()
    meas_load.wait()

    def pack(v):
        t = targ[v]
        inside = (t >= block_of * lines) & (t < (block_of + 1) * lines)
        member = jnp.where(inside, 1.0, 0.0)
        rank = jnp.dot(member.astype(bf16), before, preferred_element_type=f32)
        place = rank + (block_of * cap).astype(f32)
        slot = jnp.sum(member * place, axis=0, keepdims=True)
        first = jnp.sum(member * (block_of * lines).astype(f32), axis=0, keepdims=True)
        local = t - first.astype(jnp.int32)
        shift = rows.bit_length() - 1
        line = (local & (rows - 1)) * depth + (local >> shift)
        pick = jnp.where(slot_of == slot, 1.0, 0.0).astype(bf16)
        moved = jnp.dot(pick, meas[v], preferred_element_type=f32).astype(bf16)
        for b in range(nb):
            for g in range(nv):
                packed[b, g, v * cap:(v + 1) * cap, :] = moved[
                    b * cap:(b + 1) * cap, g * xl:(g + 1) * xl
                ]
        ids = jnp.broadcast_to((line + 1).astype(f32), (16, lines)).astype(bf16)
        ids = lax.dot_general(
            ids, pick, (((1,), (1,)), ((), ())), preferred_element_type=f32
        )
        for b in range(nb):
            idsend[b, v:v + 1, :cap] = ids[0:1, b * cap:(b + 1) * cap]

    pack(0)
    est_load.wait()
    for y in range(rows):
        est0[y] = est_in[:, y, :]

    pl.semaphore_wait(barrier, n - 1)

    def data_copy(o, v):
        b, g = peer(o)
        at = pl.ds(v * cap, cap)
        return pltpu.make_async_remote_copy(
            src_ref=packed.at[b, g, at], dst_ref=recv.at[o, at], send_sem=data_send.at[o, v],
            recv_sem=data_recv.at[o, v], device_id={"blocks": b, "views": g},
            device_id_type=MESH,
        )

    def id_copy(o):
        b, g = peer(o)
        return pltpu.make_async_remote_copy(
            src_ref=idsend.at[b], dst_ref=idrecv.at[o], send_sem=id_send.at[o],
            recv_sem=id_recv.at[o], device_id={"blocks": b, "views": g},
            device_id_type=MESH,
        )

    def halo(phase, c, src_up, dst_up, src_down, dst_down):
        up = pltpu.make_async_remote_copy(
            src_ref=src_up, dst_ref=dst_up, send_sem=hal_send.at[phase, 0, c],
            recv_sem=hal_recv.at[phase, 0, c],
            device_id={"blocks": lax.rem(my_b + 1, nb)}, device_id_type=MESH,
        )
        down = pltpu.make_async_remote_copy(
            src_ref=src_down, dst_ref=dst_down, send_sem=hal_send.at[phase, 1, c],
            recv_sem=hal_recv.at[phase, 1, c],
            device_id={"blocks": lax.rem(my_b + nb - 1, nb)}, device_id_type=MESH,
        )

        def start():
            pl.when(has_next)(up.start)
            pl.when(has_prev)(down.start)

        def arrived():
            pl.when(has_prev)(up.wait_recv)
            pl.when(has_next)(down.wait_recv)

        def sent():
            pl.when(has_next)(up.wait_send)
            pl.when(has_prev)(down.wait_send)

        return start, arrived, sent

    def est_halo(sweep, c):
        if sweep == 0:
            est, ys = est0, pl.ds(0, rows)
        else:
            est, ys = est1, pl.ds(c * per, per)
        return halo(
            2 * sweep, c,
            est.at[ys, depth - HW:depth, :], hal.at[sweep, 0, ys],
            est.at[ys, 0:HW, :], hal.at[sweep, 1, ys],
        )

    def sp_halo(sweep, c):
        ys = pl.ds(c * per, per)
        return halo(
            2 * sweep + 1, c,
            spout.at[sweep, 1, ys], spin.at[sweep, 0, ys],
            spout.at[sweep, 0, ys], spin.at[sweep, 1, ys],
        )

    each(lambda o: data_copy(o, 0).start())
    est_halo(0, 0)[0]()
    for v in range(1, vc):
        pack(v)
        if v == vc - 1:
            each(lambda o: id_copy(o).start())
        each(lambda o: data_copy(o, v).start())
    own = pltpu.make_async_copy(packed.at[my_b, my_g], recv.at[0], own_sem.at[0])
    own_id = pltpu.make_async_copy(idsend.at[my_b], idrecv.at[0], own_sem.at[1])
    own.start()
    own_id.start()

    @pl.when(my_b == 0)
    def _():
        for s in range(ITERS):
            hal[s, 0] = jnp.zeros_like(hal[s, 0])
            spin[s, 0] = jnp.zeros_like(spin[s, 0])

    @pl.when(my_b == nb - 1)
    def _():
        for s in range(ITERS):
            hal[s, 1] = jnp.zeros_like(hal[s, 1])
            spin[s, 1] = jnp.zeros_like(spin[s, 1])

    obs[...] = jnp.zeros_like(obs)
    window = depth + 2 * HW
    views, bands, taps = psf.shape
    order = [g * vc + v for v in range(vc) for g in range(nv)]
    nz = band.shape[1]
    iota = functools.partial(lax.broadcasted_iota, jnp.int32)

    band_load.wait()
    psf_load.wait()
    in_band = jnp.concatenate(
        [jnp.broadcast_to(band[v:v + 1, :], (bands, nz)) for v in range(views)], axis=0
    ) == lax.rem(iota((views * bands, nz), 0), bands)
    in_band = jnp.where(in_band, 1.0, 0.0).astype(bf16)
    reach = iota((window, nz), 1) - iota((window, nz), 0) == my_b * depth - HW
    reach = jnp.where(reach, 1.0, 0.0).astype(bf16)
    near = lax.dot_general(
        reach, in_band, (((1,), (1,)), ((), ())), preferred_element_type=f32
    )
    lane_view = iota(near.shape, 1) // bands
    near = jnp.concatenate(
        [jnp.where(lane_view == v, near, 0.0) for v in range(views)], axis=0
    ).astype(bf16)
    table = psf[...].reshape(views * bands, taps)
    found = None
    for _ in range(3):
        part = table.astype(bf16)
        table = table - part.astype(f32)
        term = jnp.dot(near, part, preferred_element_type=f32)
        found = term if found is None else found + term
    coefs[...] = jnp.zeros_like(coefs)
    for v in range(views):
        coefs[v, :, :taps] = found[v * window:(v + 1) * window]

    centre = jnp.concatenate([coefs[v, HW:HW + depth, :] for v in order], axis=0)
    row_z = lax.rem(iota(centre.shape, 0), depth)
    mat = jnp.where(row_z == 0, centre, 0.0)
    for z in range(1, depth):
        mat = mat + jnp.where(row_z == z, pltpu.roll(centre, z, 1), 0.0)
    hi = mat.astype(bf16).astype(f32)
    lo = (mat - hi).astype(bf16).astype(f32)
    triple = hi + pltpu.roll(hi, window, 1) + pltpu.roll(lo, 2 * window, 1)
    f3[...] = triple[:, :3 * window].astype(bf16)
    hi_t, lo_t = hi.T[:window], lo.T[:window]
    b3[...] = jnp.concatenate([hi_t, hi_t, lo_t], axis=1).astype(bf16)
    part_rows = nv * depth
    for v in range(vc):
        at = slice(v * part_rows, (v + 1) * part_rows)
        pad = jnp.zeros((-3 * part_rows % 128, 128), f32)
        stack = jnp.concatenate([hi[at], hi[at], lo[at], pad], axis=0)
        b3s[v] = stack.T[:window, :3 * part_rows].astype(bf16)

    both = coefs[0]
    for v in range(1, views):
        both = both + coefs[v]
    place_sum = iota(both.shape, 0) + iota(both.shape, 1)
    norm = jnp.zeros((depth, xl), f32)
    for z in range(depth):
        only = jnp.where(place_sum == z + 2 * HW, both, 0.0)
        only = jnp.sum(jnp.sum(only, axis=0, keepdims=True), axis=1, keepdims=True)
        norm = jnp.where(iota((depth, xl), 0) == z, only, norm)
    scale = 1.0 / norm
    level = jnp.concatenate([jnp.full((depth, xl), bg[v], f32) for v in order], axis=0)

    def project(sweep, est, y):
        field = jnp.concatenate([hal[sweep, 0, y], est[y], hal[sweep, 1, y]], axis=0)
        return jnp.dot(f3[...], split3(field, 0), preferred_element_type=f32) + level

    def loop(count, body):
        def step(i, carry):
            body(i)
            return carry
        lax.fori_loop(0, count, step, 0)

    est_halo(0, 0)[1]()

    def first_forward(c):
        for j in range(per):
            y = c * per + j
            fwd[y] = project(0, est0, y)

    loop(CHUNKS, first_forward)

    row_of = (lax.broadcasted_iota(jnp.int32, (lines, cap), 0) + 1).astype(f32)

    def put(o, v):
        g = xor(my_g, o % nv, nv)
        pick = jnp.where(idrecv[o, v:v + 1, :cap] == row_of, 1.0, 0.0).astype(bf16)
        found = jnp.dot(
            pick, recv[o, v * cap:(v + 1) * cap, :], preferred_element_type=f32
        ).reshape(rows, depth, xl)
        at = pl.ds(pl.multiple_of((v * nv + g) * depth, depth), depth)
        obs[:, at, :] = obs[:, at, :] + found

    def partial_back(v, y):
        at = slice(v * part_rows, (v + 1) * part_rows)
        ratio = obs[y, at, :] / fwd[y, at, :]
        part = jnp.dot(b3s[v], split3(ratio, 0), preferred_element_type=f32)
        return part if v == 0 else acc[y] + part

    own.wait()
    own_id.wait()
    for v in range(vc):
        def take(o):
            if v == 0:
                id_copy(o).wait_recv()
            data_copy(o, v).wait_recv()
            put(o, v)

        put(0, v)
        each(take)
        if v < vc - 1:
            def add(c):
                for j in range(per):
                    acc[c * per + j] = partial_back(v, c * per + j)

            loop(CHUNKS, add)

    for sweep in range(ITERS):
        est = est0 if sweep == 0 else est1

        def back(c):
            if sweep > 0:
                est_halo(sweep, c)[1]()
            for j in range(per):
                y = c * per + j
                if sweep == 0:
                    spread = partial_back(vc - 1, y)
                else:
                    ratio = obs[y] / project(sweep, est, y)
                    spread = jnp.dot(b3[...], split3(ratio, 0), preferred_element_type=f32)
                spout[sweep, 0, y] = spread[:HW]
                share[y] = spread[HW:HW + depth]
                spout[sweep, 1, y] = spread[HW + depth:]
            sp_halo(sweep, c)[0]()

        def update(c):
            sp_halo(sweep, c)[1]()
            for j in range(per):
                y = c * per + j
                total = share[y] + jnp.concatenate(
                    [spin[sweep, 0, y], spin[sweep, 1, y]], axis=0
                )
                value = est[y] * (total * scale)
                if sweep == 0:
                    est1[y] = value
                else:
                    share[y] = value
            if sweep == 0:
                est_halo(1, c)[0]()

        loop(CHUNKS, back)
        loop(CHUNKS, update)
    for y in range(rows):
        out[:, y, :] = share[y]

    def done(o):
        id_copy(o).wait_send()
        for v in range(vc):
            data_copy(o, v).wait_send()

    each(done)
    est_halo(0, 0)[2]()

    def last(c):
        sp_halo(0, c)[2]()
        est_halo(1, c)[2]()
        sp_halo(1, c)[2]()

    loop(CHUNKS, last)


def shards(nb, nv, estimate0, measured, line_target, band, psf, background):
    depth, rows, xl = estimate0.shape
    vc, _, lines, width = measured.shape
    taps, views = psf.shape[2], psf.shape[0]
    assert depth == 2 * HW and taps == 2 * HW + 1 and lines == rows * depth <= 256
    window = depth + 2 * HW
    cap = 2 * lines // nb
    n = nb * nv
    assert views * depth == 128 and 3 * window <= 128 and vc <= 8 and cap <= 128
    vz = views * depth
    vmem = pl.BlockSpec(memory_space=pltpu.VMEM)
    dma = pltpu.SemaphoreType.DMA
    return pl.pallas_call(
        functools.partial(kernel, nb, nv),
        out_shape=jax.ShapeDtypeStruct((depth, rows, xl), f32),
        in_specs=[pl.BlockSpec(memory_space=pl.ANY)] * 5 + [pl.BlockSpec(memory_space=pltpu.SMEM)],
        out_specs=vmem,
        scratch_shapes=[
            pltpu.VMEM((nb, nv, vc * cap, xl), bf16),
            pltpu.VMEM((nb, 8, 128), f32),
            pltpu.VMEM((n, vc * cap, xl), bf16),
            pltpu.VMEM((n, 8, 128), f32),
            pltpu.VMEM((rows, vz, xl), f32),
            pltpu.VMEM((rows, vz, xl), f32),
            pltpu.VMEM((rows, depth, xl), f32),
            pltpu.VMEM((rows, depth, xl), f32),
            pltpu.VMEM((rows, depth, xl), f32),
            pltpu.VMEM((ITERS, 2, rows, HW, xl), f32),
            pltpu.VMEM((ITERS, 2, rows, HW, xl), f32),
            pltpu.VMEM((ITERS, 2, rows, HW, xl), f32),
            pltpu.VMEM((vz, 3 * window), bf16),
            pltpu.VMEM((window, 3 * vz), bf16),
            pltpu.VMEM((vc, window, 3 * nv * depth), bf16),
            pltpu.VMEM((views, window, 128), f32),
            pltpu.VMEM((rows, window, xl), f32),
            pltpu.VMEM(estimate0.shape, f32),
            pltpu.VMEM((vc, lines, width), bf16),
            pltpu.VMEM(line_target.shape, jnp.int32),
            pltpu.VMEM(band.shape, jnp.int32),
            pltpu.VMEM(psf.shape, f32),
            dma((5,)),
            dma((n, vc)),
            dma((n, vc)),
            dma((n,)),
            dma((n,)),
            dma((2,)),
            dma((2 * ITERS, 2, CHUNKS)),
            dma((2 * ITERS, 2, CHUNKS)),
        ],
        compiler_params=pltpu.CompilerParams(
            collective_id=0, has_side_effects=True, vmem_limit_bytes=60 << 20
        ),
    )(estimate0, measured[:, 0], line_target, band, psf, background)


def solution(mesh):
    in_specs = (
        P(("groups", "blocks"), "sub", "views"),
        P("views", "sub", ("groups", "blocks"), None),
        P("views", "sub", ("groups", "blocks")),
        P(),
        P(),
        P(),
    )
    out_specs = P(("groups", "blocks"), "sub", "views")
    body = functools.partial(shards, mesh.shape["blocks"], mesh.shape["views"])
    return jax.shard_map(body, mesh=mesh, in_specs=in_specs, out_specs=out_specs, check_vma=False)
```

```python
import functools

import jax
import jax.numpy as jnp
from jax import lax
from jax.experimental import pallas as pl
from jax.experimental.pallas import tpu as pltpu
from jax.sharding import PartitionSpec as P

ITERS = 2
HW = 8
CHUNKS = 4
MESH = pl.DeviceIdType.MESH
f32, bf16 = jnp.float32, jnp.bfloat16


def xor(a, b, size):
    out, bit = 0, 1
    while bit < size:
        p, q = (a // bit) % 2, (b // bit) % 2
        out = out + bit * (p + q - 2 * p * q)
        bit *= 2
    return out


def split3(value, axis):
    hi = value.astype(bf16)
    lo = (value - hi.astype(f32)).astype(bf16)
    return jnp.concatenate([hi, lo, hi], axis=axis)


def kernel(
    nb, nv, est_far, meas_far, targ_far, band_far, psf_far, bg, out,
    packed, idsend, recv, idrecv, obs, fwd, est0, est1, share, hal, spout, spin, f3, b3, b3s, coefs, acc,
    est_in, meas, targ, band, psf, in_sem,
    data_send, data_recv, id_send, id_recv, own_sem, hal_send, hal_recv,
):
    vc, lines, width = meas.shape
    rows, depth, xl = est0.shape
    cap = 2 * lines // nb
    n = nb * nv
    per = rows // CHUNKS
    my_b, my_g = lax.axis_index("blocks"), lax.axis_index("views")
    has_prev, has_next = my_b > 0, my_b < nb - 1

    def each(body, near=False):
        if n <= 16:
            for o in sorted(range(1, n), key=lambda o: ((o < n // 2) != near, o % nv)):
                body(o)
        else:
            def step(i, carry):
                body(n - 1 - i)
                return carry
            lax.fori_loop(0, n - 1, step, 0)

    def peer(o):
        return xor(my_b, o // nv, nb), xor(my_g, o % nv, nv)

    barrier = pltpu.get_barrier_semaphore()

    def greet(o):
        b, g = peer(o)
        pl.semaphore_signal(
            barrier, inc=1, device_id={"blocks": b, "views": g}, device_id_type=MESH
        )

    each(greet)
    est_load, meas_load, targ_load, band_load, psf_load = [
        pltpu.make_async_copy(source, held, in_sem.at[i])
        for i, (source, held) in enumerate((
            (est_far, est_in), (meas_far, meas), (targ_far, targ), (band_far, band),
            (psf_far, psf),
        ))
    ]
    for load in (targ_load, meas_load, est_load, band_load, psf_load):
        load.start()

    idsend[...] = jnp.zeros_like(idsend)
    high = max(16, nb)
    before = (
        lax.broadcasted_iota(jnp.int32, (lines, lines), 0)
        < lax.broadcasted_iota(jnp.int32, (lines, lines), 1)
    )
    before = jnp.where(before, 1.0, 0.0).astype(bf16)
    block_of = lax.broadcasted_iota(jnp.int32, (high, lines), 0)
    slot_of = lax.broadcasted_iota(jnp.int32, (nb * cap, lines), 0).astype(f32)
    targ_load.wait()
    meas_load.wait()

    def pack(v):
        t = targ[v]
        inside = (t >= block_of * lines) & (t < (block_of + 1) * lines)
        member = jnp.where(inside, 1.0, 0.0)
        rank = jnp.dot(member.astype(bf16), before, preferred_element_type=f32)
        place = rank + (block_of * cap).astype(f32)
        slot = jnp.sum(member * place, axis=0, keepdims=True)
        first = jnp.sum(member * (block_of * lines).astype(f32), axis=0, keepdims=True)
        local = t - first.astype(jnp.int32)
        shift = rows.bit_length() - 1
        line = (local & (rows - 1)) * depth + (local >> shift)
        pick = jnp.where(slot_of == slot, 1.0, 0.0).astype(bf16)
        moved = jnp.dot(pick, meas[v], preferred_element_type=f32).astype(bf16)
        for b in range(nb):
            for g in range(nv):
                packed[b, g, v * cap:(v + 1) * cap, :] = moved[
                    b * cap:(b + 1) * cap, g * xl:(g + 1) * xl
                ]
        ids = jnp.broadcast_to((line + 1).astype(f32), (16, lines)).astype(bf16)
        ids = lax.dot_general(
            ids, pick, (((1,), (1,)), ((), ())), preferred_element_type=f32
        )
        for b in range(nb):
            idsend[b, v:v + 1, :cap] = ids[0:1, b * cap:(b + 1) * cap]

    pack(0)
    est_load.wait()
    for y in range(rows):
        est0[y] = est_in[:, y, :]

    pl.semaphore_wait(barrier, n - 1)

    def data_copy(o, v):
        b, g = peer(o)
        at = pl.ds(v * cap, cap)
        return pltpu.make_async_remote_copy(
            src_ref=packed.at[b, g, at], dst_ref=recv.at[o, at], send_sem=data_send.at[o, v],
            recv_sem=data_recv.at[o, v], device_id={"blocks": b, "views": g},
            device_id_type=MESH,
        )

    def id_copy(o):
        b, g = peer(o)
        return pltpu.make_async_remote_copy(
            src_ref=idsend.at[b], dst_ref=idrecv.at[o], send_sem=id_send.at[o],
            recv_sem=id_recv.at[o], device_id={"blocks": b, "views": g},
            device_id_type=MESH,
        )

    def halo(phase, c, src_up, dst_up, src_down, dst_down):
        up = pltpu.make_async_remote_copy(
            src_ref=src_up, dst_ref=dst_up, send_sem=hal_send.at[phase, 0, c],
            recv_sem=hal_recv.at[phase, 0, c],
            device_id={"blocks": lax.rem(my_b + 1, nb)}, device_id_type=MESH,
        )
        down = pltpu.make_async_remote_copy(
            src_ref=src_down, dst_ref=dst_down, send_sem=hal_send.at[phase, 1, c],
            recv_sem=hal_recv.at[phase, 1, c],
            device_id={"blocks": lax.rem(my_b + nb - 1, nb)}, device_id_type=MESH,
        )

        def start():
            pl.when(has_next)(up.start)
            pl.when(has_prev)(down.start)

        def arrived():
            pl.when(has_prev)(up.wait_recv)
            pl.when(has_next)(down.wait_recv)

        def sent():
            pl.when(has_next)(up.wait_send)
            pl.when(has_prev)(down.wait_send)

        return start, arrived, sent

    def est_halo(sweep, c):
        if sweep == 0:
            est, ys = est0, pl.ds(0, rows)
        else:
            est, ys = est1, pl.ds(c * per, per)
        return halo(
            2 * sweep, c,
            est.at[ys, depth - HW:depth, :], hal.at[sweep, 0, ys],
            est.at[ys, 0:HW, :], hal.at[sweep, 1, ys],
        )

    def sp_halo(sweep, c):
        ys = pl.ds(c * per, per)
        return halo(
            2 * sweep + 1, c,
            spout.at[sweep, 1, ys], spin.at[sweep, 0, ys],
            spout.at[sweep, 0, ys], spin.at[sweep, 1, ys],
        )

    each(lambda o: data_copy(o, 0).start())
    est_halo(0, 0)[0]()
    for v in range(1, vc):
        pack(v)
        if v == vc - 1:
            each(lambda o: id_copy(o).start())
        each(lambda o: data_copy(o, v).start())
    own = pltpu.make_async_copy(packed.at[my_b, my_g], recv.at[0], own_sem.at[0])
    own_id = pltpu.make_async_copy(idsend.at[my_b], idrecv.at[0], own_sem.at[1])
    own.start()
    own_id.start()

    @pl.when(my_b == 0)
    def _():
        for s in range(ITERS):
            hal[s, 0] = jnp.zeros_like(hal[s, 0])
            spin[s, 0] = jnp.zeros_like(spin[s, 0])

    @pl.when(my_b == nb - 1)
    def _():
        for s in range(ITERS):
            hal[s, 1] = jnp.zeros_like(hal[s, 1])
            spin[s, 1] = jnp.zeros_like(spin[s, 1])

    obs[...] = jnp.zeros_like(obs)
    window = depth + 2 * HW
    views, bands, taps = psf.shape
    order = [g * vc + v for v in range(vc) for g in range(nv)]
    nz = band.shape[1]
    iota = functools.partial(lax.broadcasted_iota, jnp.int32)

    band_load.wait()
    psf_load.wait()
    in_band = jnp.concatenate(
        [jnp.broadcast_to(band[v:v + 1, :], (bands, nz)) for v in range(views)], axis=0
    ) == lax.rem(iota((views * bands, nz), 0), bands)
    in_band = jnp.where(in_band, 1.0, 0.0).astype(bf16)
    reach = iota((window, nz), 1) - iota((window, nz), 0) == my_b * depth - HW
    reach = jnp.where(reach, 1.0, 0.0).astype(bf16)
    near = lax.dot_general(
        reach, in_band, (((1,), (1,)), ((), ())), preferred_element_type=f32
    )
    lane_view = iota(near.shape, 1) // bands
    near = jnp.concatenate(
        [jnp.where(lane_view == v, near, 0.0) for v in range(views)], axis=0
    ).astype(bf16)
    table = psf[...].reshape(views * bands, taps)
    found = None
    for _ in range(3):
        part = table.astype(bf16)
        table = table - part.astype(f32)
        term = jnp.dot(near, part, preferred_element_type=f32)
        found = term if found is None else found + term
    coefs[...] = jnp.zeros_like(coefs)
    for v in range(views):
        coefs[v, :, :taps] = found[v * window:(v + 1) * window]

    centre = jnp.concatenate([coefs[v, HW:HW + depth, :] for v in order], axis=0)
    row_z = lax.rem(iota(centre.shape, 0), depth)
    mat = jnp.where(row_z == 0, centre, 0.0)
    for z in range(1, depth):
        mat = mat + jnp.where(row_z == z, pltpu.roll(centre, z, 1), 0.0)
    hi = mat.astype(bf16).astype(f32)
    lo = (mat - hi).astype(bf16).astype(f32)
    triple = hi + pltpu.roll(hi, window, 1) + pltpu.roll(lo, 2 * window, 1)
    f3[...] = triple[:, :3 * window].astype(bf16)
    hi_t, lo_t = hi.T[:window], lo.T[:window]
    b3[...] = jnp.concatenate([hi_t, hi_t, lo_t], axis=1).astype(bf16)
    part_rows = nv * depth
    for v in range(vc):
        at = slice(v * part_rows, (v + 1) * part_rows)
        pad = jnp.zeros((-3 * part_rows % 128, 128), f32)
        stack = jnp.concatenate([hi[at], hi[at], lo[at], pad], axis=0)
        b3s[v] = stack.T[:window, :3 * part_rows].astype(bf16)

    both = coefs[0]
    for v in range(1, views):
        both = both + coefs[v]
    place_sum = iota(both.shape, 0) + iota(both.shape, 1)
    norm = jnp.zeros((depth, xl), f32)
    for z in range(depth):
        only = jnp.where(place_sum == z + 2 * HW, both, 0.0)
        only = jnp.sum(jnp.sum(only, axis=0, keepdims=True), axis=1, keepdims=True)
        norm = jnp.where(iota((depth, xl), 0) == z, only, norm)
    scale = 1.0 / norm
    level = jnp.concatenate([jnp.full((depth, xl), bg[v], f32) for v in order], axis=0)

    def project(sweep, est, y):
        field = jnp.concatenate([hal[sweep, 0, y], est[y], hal[sweep, 1, y]], axis=0)
        return jnp.dot(f3[...], split3(field, 0), preferred_element_type=f32) + level

    def loop(count, body):
        def step(i, carry):
            body(i)
            return carry
        lax.fori_loop(0, count, step, 0)

    est_halo(0, 0)[1]()

    def first_forward(c):
        for j in range(per):
            y = c * per + j
            fwd[y] = project(0, est0, y)

    loop(CHUNKS, first_forward)

    row_of = (lax.broadcasted_iota(jnp.int32, (lines, cap), 0) + 1).astype(f32)

    def put(o, v):
        g = xor(my_g, o % nv, nv)
        pick = jnp.where(idrecv[o, v:v + 1, :cap] == row_of, 1.0, 0.0).astype(bf16)
        found = jnp.dot(
            pick, recv[o, v * cap:(v + 1) * cap, :], preferred_element_type=f32
        ).reshape(rows, depth, xl)
        at = pl.ds(pl.multiple_of((v * nv + g) * depth, depth), depth)
        obs[:, at, :] = obs[:, at, :] + found

    def partial_back(v, y):
        at = slice(v * part_rows, (v + 1) * part_rows)
        ratio = obs[y, at, :] / fwd[y, at, :]
        part = jnp.dot(b3s[v], split3(ratio, 0), preferred_element_type=f32)
        return part if v == 0 else acc[y] + part

    own.wait()
    own_id.wait()
    for v in range(vc):
        def take(o):
            if v == 0:
                id_copy(o).wait_recv()
            data_copy(o, v).wait_recv()
            put(o, v)

        put(0, v)
        each(take, near=True)
        if v < vc - 1:
            def add(c):
                for j in range(per):
                    acc[c * per + j] = partial_back(v, c * per + j)

            loop(CHUNKS, add)

    for sweep in range(ITERS):
        est = est0 if sweep == 0 else est1

        def back(c):
            if sweep > 0:
                est_halo(sweep, c)[1]()
            for j in range(per):
                y = c * per + j
                if sweep == 0:
                    spread = partial_back(vc - 1, y)
                else:
                    ratio = obs[y] / project(sweep, est, y)
                    spread = jnp.dot(b3[...], split3(ratio, 0), preferred_element_type=f32)
                spout[sweep, 0, y] = spread[:HW]
                share[y] = spread[HW:HW + depth]
                spout[sweep, 1, y] = spread[HW + depth:]
            sp_halo(sweep, c)[0]()

        def update(c):
            sp_halo(sweep, c)[1]()
            for j in range(per):
                y = c * per + j
                total = share[y] + jnp.concatenate(
                    [spin[sweep, 0, y], spin[sweep, 1, y]], axis=0
                )
                value = est[y] * (total * scale)
                if sweep == 0:
                    est1[y] = value
                else:
                    share[y] = value
            if sweep == 0:
                est_halo(1, c)[0]()

        loop(CHUNKS, back)
        loop(CHUNKS, update)
    for y in range(rows):
        out[:, y, :] = share[y]

    def done(o):
        id_copy(o).wait_send()
        for v in range(vc):
            data_copy(o, v).wait_send()

    each(done)
    est_halo(0, 0)[2]()

    def last(c):
        sp_halo(0, c)[2]()
        est_halo(1, c)[2]()
        sp_halo(1, c)[2]()

    loop(CHUNKS, last)


def shards(nb, nv, estimate0, measured, line_target, band, psf, background):
    depth, rows, xl = estimate0.shape
    vc, _, lines, width = measured.shape
    taps, views = psf.shape[2], psf.shape[0]
    assert depth == 2 * HW and taps == 2 * HW + 1 and lines == rows * depth <= 256
    window = depth + 2 * HW
    cap = 2 * lines // nb
    n = nb * nv
    assert views * depth == 128 and 3 * window <= 128 and vc <= 8 and cap <= 128
    vz = views * depth
    vmem = pl.BlockSpec(memory_space=pltpu.VMEM)
    dma = pltpu.SemaphoreType.DMA
    return pl.pallas_call(
        functools.partial(kernel, nb, nv),
        out_shape=jax.ShapeDtypeStruct((depth, rows, xl), f32),
        in_specs=[pl.BlockSpec(memory_space=pl.ANY)] * 5 + [pl.BlockSpec(memory_space=pltpu.SMEM)],
        out_specs=vmem,
        scratch_shapes=[
            pltpu.VMEM((nb, nv, vc * cap, xl), bf16),
            pltpu.VMEM((nb, 8, 128), f32),
            pltpu.VMEM((n, vc * cap, xl), bf16),
            pltpu.VMEM((n, 8, 128), f32),
            pltpu.VMEM((rows, vz, xl), f32),
            pltpu.VMEM((rows, vz, xl), f32),
            pltpu.VMEM((rows, depth, xl), f32),
            pltpu.VMEM((rows, depth, xl), f32),
            pltpu.VMEM((rows, depth, xl), f32),
            pltpu.VMEM((ITERS, 2, rows, HW, xl), f32),
            pltpu.VMEM((ITERS, 2, rows, HW, xl), f32),
            pltpu.VMEM((ITERS, 2, rows, HW, xl), f32),
            pltpu.VMEM((vz, 3 * window), bf16),
            pltpu.VMEM((window, 3 * vz), bf16),
            pltpu.VMEM((vc, window, 3 * nv * depth), bf16),
            pltpu.VMEM((views, window, 128), f32),
            pltpu.VMEM((rows, window, xl), f32),
            pltpu.VMEM(estimate0.shape, f32),
            pltpu.VMEM((vc, lines, width), bf16),
            pltpu.VMEM(line_target.shape, jnp.int32),
            pltpu.VMEM(band.shape, jnp.int32),
            pltpu.VMEM(psf.shape, f32),
            dma((5,)),
            dma((n, vc)),
            dma((n, vc)),
            dma((n,)),
            dma((n,)),
            dma((2,)),
            dma((2 * ITERS, 2, CHUNKS)),
            dma((2 * ITERS, 2, CHUNKS)),
        ],
        compiler_params=pltpu.CompilerParams(
            collective_id=0, has_side_effects=True, vmem_limit_bytes=60 << 20
        ),
    )(estimate0, measured[:, 0], line_target, band, psf, background)


def solution(mesh):
    in_specs = (
        P(("groups", "blocks"), "sub", "views"),
        P("views", "sub", ("groups", "blocks"), None),
        P("views", "sub", ("groups", "blocks")),
        P(),
        P(),
        P(),
    )
    out_specs = P(("groups", "blocks"), "sub", "views")
    body = functools.partial(shards, mesh.shape["blocks"], mesh.shape["views"])
    return jax.shard_map(body, mesh=mesh, in_specs=in_specs, out_specs=out_specs, check_vma=False)
```

```python
import functools

import jax
import jax.numpy as jnp
from jax import lax
from jax.experimental import pallas as pl
from jax.experimental.pallas import tpu as pltpu
from jax.sharding import PartitionSpec as P

ITERS = 2
HW = 8
CHUNKS = 4
MESH = pl.DeviceIdType.MESH
f32, bf16 = jnp.float32, jnp.bfloat16


def xor(a, b, size):
    out, bit = 0, 1
    while bit < size:
        p, q = (a // bit) % 2, (b // bit) % 2
        out = out + bit * (p + q - 2 * p * q)
        bit *= 2
    return out


def split3(value, axis):
    hi = value.astype(bf16)
    lo = (value - hi.astype(f32)).astype(bf16)
    return jnp.concatenate([hi, lo, hi], axis=axis)


def kernel(
    nb, nv, est_far, meas_far, targ_far, band_far, psf_far, bg, out,
    packed, idsend, recv, idrecv, obs, fwd, est0, est1, share, hal, spout, spin, f3, b3, b3s, coefs, acc,
    est_in, meas, targ, band, psf, in_sem,
    data_send, data_recv, id_send, id_recv, own_sem, hal_send, hal_recv,
):
    vc, lines, width = meas.shape
    rows, depth, xl = est0.shape
    cap = 2 * lines // nb
    n = nb * nv
    per = rows // CHUNKS
    my_b, my_g = lax.axis_index("blocks"), lax.axis_index("views")
    has_prev, has_next = my_b > 0, my_b < nb - 1

    def each(body, near=False):
        if n <= 16:
            for o in sorted(range(1, n), key=lambda o: ((o < n // 2) != near, o % nv)):
                body(o)
        else:
            def step(i, carry):
                body(n - 1 - i)
                return carry
            lax.fori_loop(0, n - 1, step, 0)

    def peer(o):
        return xor(my_b, o // nv, nb), xor(my_g, o % nv, nv)

    barrier = pltpu.get_barrier_semaphore()

    def greet(o):
        b, g = peer(o)
        pl.semaphore_signal(
            barrier, inc=1, device_id={"blocks": b, "views": g}, device_id_type=MESH
        )

    each(greet)
    est_load, meas_load, targ_load, band_load, psf_load = [
        pltpu.make_async_copy(source, held, in_sem.at[i])
        for i, (source, held) in enumerate((
            (est_far, est_in), (meas_far, meas), (targ_far, targ), (band_far, band),
            (psf_far, psf),
        ))
    ]
    for load in (targ_load, meas_load, est_load, band_load, psf_load):
        load.start()

    idsend[...] = jnp.zeros_like(idsend)
    high = max(16, nb)
    before = (
        lax.broadcasted_iota(jnp.int32, (lines, lines), 0)
        < lax.broadcasted_iota(jnp.int32, (lines, lines), 1)
    )
    before = jnp.where(before, 1.0, 0.0).astype(bf16)
    block_of = lax.broadcasted_iota(jnp.int32, (high, lines), 0)
    slot_of = lax.broadcasted_iota(jnp.int32, (nb * cap, lines), 0).astype(f32)
    targ_load.wait()
    meas_load.wait()

    def pack(v):
        t = targ[v]
        inside = (t >= block_of * lines) & (t < (block_of + 1) * lines)
        member = jnp.where(inside, 1.0, 0.0)
        rank = jnp.dot(member.astype(bf16), before, preferred_element_type=f32)
        place = rank + (block_of * cap).astype(f32)
        slot = jnp.sum(member * place, axis=0, keepdims=True)
        first = jnp.sum(member * (block_of * lines).astype(f32), axis=0, keepdims=True)
        local = t - first.astype(jnp.int32)
        shift = rows.bit_length() - 1
        line = (local & (rows - 1)) * depth + (local >> shift)
        pick = jnp.where(slot_of == slot, 1.0, 0.0).astype(bf16)
        moved = jnp.dot(pick, meas[v], preferred_element_type=f32).astype(bf16)
        for b in range(nb):
            for g in range(nv):
                packed[b, g, v * cap:(v + 1) * cap, :] = moved[
                    b * cap:(b + 1) * cap, g * xl:(g + 1) * xl
                ]
        ids = jnp.broadcast_to((line + 1).astype(f32), (16, lines)).astype(bf16)
        ids = lax.dot_general(
            ids, pick, (((1,), (1,)), ((), ())), preferred_element_type=f32
        )
        for b in range(nb):
            idsend[b, v:v + 1, :cap] = ids[0:1, b * cap:(b + 1) * cap]

    pack(0)
    est_load.wait()
    for y in range(rows):
        est0[y] = est_in[:, y, :]

    pl.semaphore_wait(barrier, n - 1)

    def data_copy(o, v):
        b, g = peer(o)
        at = pl.ds(v * cap, cap)
        return pltpu.make_async_remote_copy(
            src_ref=packed.at[b, g, at], dst_ref=recv.at[o, at], send_sem=data_send.at[o, v],
            recv_sem=data_recv.at[o, v], device_id={"blocks": b, "views": g},
            device_id_type=MESH,
        )

    def id_copy(o):
        b, g = peer(o)
        return pltpu.make_async_remote_copy(
            src_ref=idsend.at[b], dst_ref=idrecv.at[o], send_sem=id_send.at[o],
            recv_sem=id_recv.at[o], device_id={"blocks": b, "views": g},
            device_id_type=MESH,
        )

    def halo(phase, c, src_up, dst_up, src_down, dst_down):
        up = pltpu.make_async_remote_copy(
            src_ref=src_up, dst_ref=dst_up, send_sem=hal_send.at[phase, 0, c],
            recv_sem=hal_recv.at[phase, 0, c],
            device_id={"blocks": lax.rem(my_b + 1, nb)}, device_id_type=MESH,
        )
        down = pltpu.make_async_remote_copy(
            src_ref=src_down, dst_ref=dst_down, send_sem=hal_send.at[phase, 1, c],
            recv_sem=hal_recv.at[phase, 1, c],
            device_id={"blocks": lax.rem(my_b + nb - 1, nb)}, device_id_type=MESH,
        )

        def start():
            pl.when(has_next)(up.start)
            pl.when(has_prev)(down.start)

        def arrived():
            pl.when(has_prev)(up.wait_recv)
            pl.when(has_next)(down.wait_recv)

        def sent():
            pl.when(has_next)(up.wait_send)
            pl.when(has_prev)(down.wait_send)

        return start, arrived, sent

    def est_halo(sweep, c):
        if sweep == 0:
            est, ys = est0, pl.ds(0, rows)
        else:
            est, ys = est1, pl.ds(c * per, per)
        return halo(
            2 * sweep, c,
            est.at[ys, depth - HW:depth, :], hal.at[sweep, 0, ys],
            est.at[ys, 0:HW, :], hal.at[sweep, 1, ys],
        )

    def sp_halo(sweep, c):
        ys = pl.ds(c * per, per)
        return halo(
            2 * sweep + 1, c,
            spout.at[sweep, 1, ys], spin.at[sweep, 0, ys],
            spout.at[sweep, 0, ys], spin.at[sweep, 1, ys],
        )

    est_halo(0, 0)[0]()
    each(lambda o: data_copy(o, 0).start())
    for v in range(1, vc):
        pack(v)
        if v == vc - 1:
            each(lambda o: id_copy(o).start())
        each(lambda o: data_copy(o, v).start())
    own = pltpu.make_async_copy(packed.at[my_b, my_g], recv.at[0], own_sem.at[0])
    own_id = pltpu.make_async_copy(idsend.at[my_b], idrecv.at[0], own_sem.at[1])
    own.start()
    own_id.start()

    @pl.when(my_b == 0)
    def _():
        for s in range(ITERS):
            hal[s, 0] = jnp.zeros_like(hal[s, 0])
            spin[s, 0] = jnp.zeros_like(spin[s, 0])

    @pl.when(my_b == nb - 1)
    def _():
        for s in range(ITERS):
            hal[s, 1] = jnp.zeros_like(hal[s, 1])
            spin[s, 1] = jnp.zeros_like(spin[s, 1])

    obs[...] = jnp.zeros_like(obs)
    window = depth + 2 * HW
    views, bands, taps = psf.shape
    order = [g * vc + v for v in range(vc) for g in range(nv)]
    nz = band.shape[1]
    iota = functools.partial(lax.broadcasted_iota, jnp.int32)

    band_load.wait()
    psf_load.wait()
    in_band = jnp.concatenate(
        [jnp.broadcast_to(band[v:v + 1, :], (bands, nz)) for v in range(views)], axis=0
    ) == lax.rem(iota((views * bands, nz), 0), bands)
    in_band = jnp.where(in_band, 1.0, 0.0).astype(bf16)
    reach = iota((window, nz), 1) - iota((window, nz), 0) == my_b * depth - HW
    reach = jnp.where(reach, 1.0, 0.0).astype(bf16)
    near = lax.dot_general(
        reach, in_band, (((1,), (1,)), ((), ())), preferred_element_type=f32
    )
    lane_view = iota(near.shape, 1) // bands
    near = jnp.concatenate(
        [jnp.where(lane_view == v, near, 0.0) for v in range(views)], axis=0
    ).astype(bf16)
    table = psf[...].reshape(views * bands, taps)
    found = None
    for _ in range(3):
        part = table.astype(bf16)
        table = table - part.astype(f32)
        term = jnp.dot(near, part, preferred_element_type=f32)
        found = term if found is None else found + term
    coefs[...] = jnp.zeros_like(coefs)
    for v in range(views):
        coefs[v, :, :taps] = found[v * window:(v + 1) * window]

    centre = jnp.concatenate([coefs[v, HW:HW + depth, :] for v in order], axis=0)
    row_z = lax.rem(iota(centre.shape, 0), depth)
    mat = jnp.where(row_z == 0, centre, 0.0)
    for z in range(1, depth):
        mat = mat + jnp.where(row_z == z, pltpu.roll(centre, z, 1), 0.0)
    hi = mat.astype(bf16).astype(f32)
    lo = (mat - hi).astype(bf16).astype(f32)
    triple = hi + pltpu.roll(hi, window, 1) + pltpu.roll(lo, 2 * window, 1)
    f3[...] = triple[:, :3 * window].astype(bf16)
    hi_t, lo_t = hi.T[:window], lo.T[:window]
    b3[...] = jnp.concatenate([hi_t, hi_t, lo_t], axis=1).astype(bf16)
    part_rows = nv * depth
    for v in range(vc):
        at = slice(v * part_rows, (v + 1) * part_rows)
        pad = jnp.zeros((-3 * part_rows % 128, 128), f32)
        stack = jnp.concatenate([hi[at], hi[at], lo[at], pad], axis=0)
        b3s[v] = stack.T[:window, :3 * part_rows].astype(bf16)

    both = coefs[0]
    for v in range(1, views):
        both = both + coefs[v]
    place_sum = iota(both.shape, 0) + iota(both.shape, 1)
    norm = jnp.zeros((depth, xl), f32)
    for z in range(depth):
        only = jnp.where(place_sum == z + 2 * HW, both, 0.0)
        only = jnp.sum(jnp.sum(only, axis=0, keepdims=True), axis=1, keepdims=True)
        norm = jnp.where(iota((depth, xl), 0) == z, only, norm)
    scale = 1.0 / norm
    level = jnp.concatenate([jnp.full((depth, xl), bg[v], f32) for v in order], axis=0)

    def project(sweep, est, y):
        field = jnp.concatenate([hal[sweep, 0, y], est[y], hal[sweep, 1, y]], axis=0)
        return jnp.dot(f3[...], split3(field, 0), preferred_element_type=f32) + level

    def loop(count, body):
        def step(i, carry):
            body(i)
            return carry
        lax.fori_loop(0, count, step, 0)

    est_halo(0, 0)[1]()

    def first_forward(c):
        for j in range(per):
            y = c * per + j
            fwd[y] = project(0, est0, y)

    loop(CHUNKS, first_forward)

    row_of = (lax.broadcasted_iota(jnp.int32, (lines, cap), 0) + 1).astype(f32)

    def put(o, v):
        g = xor(my_g, o % nv, nv)
        pick = jnp.where(idrecv[o, v:v + 1, :cap] == row_of, 1.0, 0.0).astype(bf16)
        found = jnp.dot(
            pick, recv[o, v * cap:(v + 1) * cap, :], preferred_element_type=f32
        ).reshape(rows, depth, xl)
        at = pl.ds(pl.multiple_of((v * nv + g) * depth, depth), depth)
        obs[:, at, :] = obs[:, at, :] + found

    def partial_back(v, y):
        at = slice(v * part_rows, (v + 1) * part_rows)
        ratio = obs[y, at, :] / fwd[y, at, :]
        part = jnp.dot(b3s[v], split3(ratio, 0), preferred_element_type=f32)
        return part if v == 0 else acc[y] + part

    own.wait()
    own_id.wait()
    for v in range(vc):
        def take(o):
            if v == 0:
                id_copy(o).wait_recv()
            data_copy(o, v).wait_recv()
            put(o, v)

        put(0, v)
        each(take, near=True)
        if v < vc - 1:
            def add(c):
                for j in range(per):
                    acc[c * per + j] = partial_back(v, c * per + j)

            loop(CHUNKS, add)

    for sweep in range(ITERS):
        est = est0 if sweep == 0 else est1

        def back(c):
            if sweep > 0:
                est_halo(sweep, c)[1]()
            for j in range(per):
                y = c * per + j
                if sweep == 0:
                    spread = partial_back(vc - 1, y)
                else:
                    ratio = obs[y] / project(sweep, est, y)
                    spread = jnp.dot(b3[...], split3(ratio, 0), preferred_element_type=f32)
                spout[sweep, 0, y] = spread[:HW]
                share[y] = spread[HW:HW + depth]
                spout[sweep, 1, y] = spread[HW + depth:]
            sp_halo(sweep, c)[0]()

        def update(c):
            sp_halo(sweep, c)[1]()
            for j in range(per):
                y = c * per + j
                total = share[y] + jnp.concatenate(
                    [spin[sweep, 0, y], spin[sweep, 1, y]], axis=0
                )
                value = est[y] * (total * scale)
                if sweep == 0:
                    est1[y] = value
                else:
                    share[y] = value
            if sweep == 0:
                est_halo(1, c)[0]()

        loop(CHUNKS, back)
        loop(CHUNKS, update)
    for y in range(rows):
        out[:, y, :] = share[y]

    def done(o):
        id_copy(o).wait_send()
        for v in range(vc):
            data_copy(o, v).wait_send()

    each(done)
    est_halo(0, 0)[2]()

    def last(c):
        sp_halo(0, c)[2]()
        est_halo(1, c)[2]()
        sp_halo(1, c)[2]()

    loop(CHUNKS, last)


def shards(nb, nv, estimate0, measured, line_target, band, psf, background):
    depth, rows, xl = estimate0.shape
    vc, _, lines, width = measured.shape
    taps, views = psf.shape[2], psf.shape[0]
    assert depth == 2 * HW and taps == 2 * HW + 1 and lines == rows * depth <= 256
    window = depth + 2 * HW
    cap = 2 * lines // nb
    n = nb * nv
    assert views * depth == 128 and 3 * window <= 128 and vc <= 8 and cap <= 128
    vz = views * depth
    vmem = pl.BlockSpec(memory_space=pltpu.VMEM)
    dma = pltpu.SemaphoreType.DMA
    return pl.pallas_call(
        functools.partial(kernel, nb, nv),
        out_shape=jax.ShapeDtypeStruct((depth, rows, xl), f32),
        in_specs=[pl.BlockSpec(memory_space=pl.ANY)] * 5 + [pl.BlockSpec(memory_space=pltpu.SMEM)],
        out_specs=vmem,
        scratch_shapes=[
            pltpu.VMEM((nb, nv, vc * cap, xl), bf16),
            pltpu.VMEM((nb, 8, 128), f32),
            pltpu.VMEM((n, vc * cap, xl), bf16),
            pltpu.VMEM((n, 8, 128), f32),
            pltpu.VMEM((rows, vz, xl), f32),
            pltpu.VMEM((rows, vz, xl), f32),
            pltpu.VMEM((rows, depth, xl), f32),
            pltpu.VMEM((rows, depth, xl), f32),
            pltpu.VMEM((rows, depth, xl), f32),
            pltpu.VMEM((ITERS, 2, rows, HW, xl), f32),
            pltpu.VMEM((ITERS, 2, rows, HW, xl), f32),
            pltpu.VMEM((ITERS, 2, rows, HW, xl), f32),
            pltpu.VMEM((vz, 3 * window), bf16),
            pltpu.VMEM((window, 3 * vz), bf16),
            pltpu.VMEM((vc, window, 3 * nv * depth), bf16),
            pltpu.VMEM((views, window, 128), f32),
            pltpu.VMEM((rows, window, xl), f32),
            pltpu.VMEM(estimate0.shape, f32),
            pltpu.VMEM((vc, lines, width), bf16),
            pltpu.VMEM(line_target.shape, jnp.int32),
            pltpu.VMEM(band.shape, jnp.int32),
            pltpu.VMEM(psf.shape, f32),
            dma((5,)),
            dma((n, vc)),
            dma((n, vc)),
            dma((n,)),
            dma((n,)),
            dma((2,)),
            dma((2 * ITERS, 2, CHUNKS)),
            dma((2 * ITERS, 2, CHUNKS)),
        ],
        compiler_params=pltpu.CompilerParams(
            collective_id=0, has_side_effects=True, vmem_limit_bytes=60 << 20
        ),
    )(estimate0, measured[:, 0], line_target, band, psf, background)


def solution(mesh):
    in_specs = (
        P(("groups", "blocks"), "sub", "views"),
        P("views", "sub", ("groups", "blocks"), None),
        P("views", "sub", ("groups", "blocks")),
        P(),
        P(),
        P(),
    )
    out_specs = P(("groups", "blocks"), "sub", "views")
    body = functools.partial(shards, mesh.shape["blocks"], mesh.shape["views"])
    return jax.shard_map(body, mesh=mesh, in_specs=in_specs, out_specs=out_specs, check_vma=False)
```
